256 devices in a mesh: filt: 16 (over z_hi, x, core), slab: 16 (over y, z_lo).
Axes of the slice: x: 4, y: 4, z: 8 (z_hi: 2, z_lo: 4; z = z_hi * 4 + z_lo), core: 2. Of those that a mesh axis runs over, the one named last changes fastest.
Arguments:
- inputs: bfloat16 [1024, 16, 1024], P('filt', 'slab'), may hold values from -6 to 6
- weights: bfloat16 [1024, 27, 1024], P('filt', None, 'slab'), may hold values from -0.0390625 to 0.0390625
- bias: bfloat16 [1024], P('filt'), may hold values from -3 to 3
- cotangent: bfloat16 [1024, 16, 1024], P('filt', 'slab'), may hold values from -6 to 6
Outputs:
- activated: bfloat16 [1024, 16, 1024], P('filt', 'slab')
- input_grad: bfloat16 [1024, 16, 1024], P('filt', 'slab')
The draws below stay inside these ranges and needn't reach their ends.
All inputs are finite; a program needn't handle non-finite values.
Results may differ from the reference program's by a relative error of at most 0.019.
Values may be sent and summed in bfloat16 or wider, within the bound.
No kernel may reach another device: no remote copies, remote signals or barrier semaphores. Data moves between devices by JAX's collectives and lax.ppermute only.
A program may use at most 256 MiB of HBM per device.

```python
import jax
import jax.numpy as jnp
from jax import lax

CIN = 1024
COUT = 1024
TAPS = 27
HH = 32
WW = 32
DEPTH = 16


def block_scale(own_key, extent, shards, smallest, top_value):
    gain, own = 1.0, jax.random.fold_in(own_key, 6)
    for axis_at, shards_of in shards:
        steps = jnp.exp(jax.random.uniform(jax.random.fold_in(own, axis_at), (shards_of,), jnp.float32, smallest / len(shards), top_value / len(shards)))
        gain = gain * jnp.repeat(steps, extent[axis_at] // shards_of).reshape([-1 if axis == axis_at else 1 for axis in range(len(extent))])
    return gain


def noise(rng, dims, deviation, limit, split=(), dtype=jnp.bfloat16):
    values = jax.random.normal(rng, dims, jnp.float32) * deviation
    if len(split) > 0:
        values = block_scale(rng, dims, split, -0.22, 0.18) * values
    return jnp.clip(values, min=-limit, max=limit).astype(dtype)


def setup_inputs(seed: int = 0) -> dict:
    key_list = jax.random.split(jax.random.key(seed), 5)
    return {
        "inputs": noise(key_list[0], (CIN, DEPTH, HH * WW), 1.0, 6.0, ((0, 16), (1, 16))),
        "weights": noise(key_list[1], (COUT, TAPS, CIN), (TAPS * CIN) ** -0.5, 0.0390625, ((0, 16), (2, 16))),
        "bias": noise(key_list[2], (COUT,), 0.5, 3.0, ((0, 16),)),
        "cotangent": noise(key_list[3], (COUT, DEPTH, HH * WW), 1.0, 6.0, ((0, 16), (1, 16))),
    }


tap_shifts = [(a - 1, b - 1, c - 1) for a in range(3) for b in range(3) for c in range(3)]


def padded_volume(block):
    volume = block.reshape(block.shape[0], block.shape[1], HH, WW)
    return jnp.pad(volume, ((0, 0), (1, 1), (1, 1), (1, 1)))


def tap_block(padded, step_depth, step_row, step_col, planes):
    window = padded[:, 1 + step_depth:1 + step_depth + planes, 1 + step_row:1 + step_row + HH, 1 + step_col:1 + step_col + WW]
    return window.reshape(padded.shape[0], planes * HH * WW)


def silu_slope(value):
    sig = jax.nn.sigmoid(value)
    return sig * (1.0 + value * (1.0 - sig))


def reference(inputs, weights, bias, cotangent):
    planes = inputs.shape[1]
    padded = padded_volume(inputs)
    preact = jnp.zeros((COUT, planes * HH * WW), jnp.float32)
    for index in range(len(tap_shifts)):
        shift_set = tap_shifts[index]
        moved = tap_block(padded, shift_set[0], shift_set[1], shift_set[2], planes).astype(jnp.float32)
        preact = preact + jnp.dot(weights[:, index, :].astype(jnp.float32), moved, precision=lax.Precision.HIGHEST, preferred_element_type=jnp.float32)
    preact = preact + bias.astype(jnp.float32)[:, None]
    activated = jax.nn.silu(preact).astype(jnp.bfloat16).reshape(COUT, planes, HH * WW)
    grad_pre = (cotangent.reshape(COUT, planes * HH * WW).astype(jnp.float32) * silu_slope(preact)).astype(jnp.bfloat16)
    padded_grad = padded_volume(grad_pre.reshape(COUT, planes, HH * WW))
    summed = jnp.zeros((CIN, planes * HH * WW), jnp.float32)
    for index in range(len(tap_shifts)):
        shift_set = tap_shifts[index]
        moved = tap_block(padded_grad, -shift_set[0], -shift_set[1], -shift_set[2], planes).astype(jnp.float32)
        summed = summed + jnp.dot(weights[:, index, :].astype(jnp.float32).T, moved, precision=lax.Precision.HIGHEST, preferred_element_type=jnp.float32)
    input_grad = summed.astype(jnp.bfloat16).reshape(CIN, planes, HH * WW)
    return activated, input_grad
```

```python
import functools

import jax
import jax.numpy as jnp
from jax import lax
from jax.experimental import pallas as pl
from jax.experimental.pallas import tpu as pltpu
from jax.sharding import PartitionSpec as P

HH = 32
WW = 32
CELLS = HH * WW
TAPS = 27
SLOTS = 28
BLOCK = 64
COLS = SLOTS * BLOCK
HALF = COLS // 2
BLOCKS = 16
CHANNELS = BLOCKS * BLOCK

ZH, XN, CN = 2, 4, 2
YN, ZN = 4, 4

BF16 = jnp.bfloat16
F32 = jnp.float32
LIMIT = pltpu.CompilerParams(vmem_limit_bytes=48 * 1024 * 1024)


def filt_index(zh, x, c):
    return (zh * XN + x) * CN + c


FILT = [(zh, x, c) for zh in range(ZH) for x in range(XN) for c in range(CN)]
SLAB = [(y, z) for y in range(YN) for z in range(ZN)]
TO_CORE = [(filt_index(*d), filt_index(d[0], d[1], 1 - d[2])) for d in FILT]
TO_ZHI = [(filt_index(*d), filt_index(1 - d[0], d[1], d[2])) for d in FILT]


def to_x(k):
    return [(filt_index(*d), filt_index(d[0], (d[1] + k) % XN, d[2])) for d in FILT]


def to_y(k):
    return [(y * ZN + z, ((y + k) % YN) * ZN + z) for y, z in SLAB]


def to_z(k):
    return [(y * ZN + z, y * ZN + (z + k) % ZN) for y, z in SLAB]


UP = [(i, i + 1) for i in range(YN * ZN - 1)]
DOWN = [(i + 1, i) for i in range(YN * ZN - 1)]

VMEM = pl.BlockSpec(memory_space=pltpu.VMEM)
ANY = pl.BlockSpec(memory_space=pl.ANY)


def transpose_kernel(w_ref, out_ref):
    rows = TAPS * BLOCK
    for start in range(0, rows, 128):
        size = min(128, rows - start)
        part = w_ref[start : start + size, :].astype(F32)
        if size < 128:
            part = jnp.concatenate([part, jnp.zeros((128 - size, BLOCK), F32)], axis=0)
        out_ref[:, start : start + 128] = part.T.astype(BF16)


def filt_position():
    mine = lax.axis_index("filt")
    return mine // (XN * CN), (mine // CN) % XN, mine % CN


def slab_position():
    mine = lax.axis_index("slab")
    return mine // ZN, mine % ZN


def weight_copies(refs, scratch, sem, place):
    y, z = slab_position()
    copies = []
    for step_y in range(YN):
        for step_z in range(ZN):
            block = ((y + YN - step_y) % YN) * ZN + (z + ZN - step_z) % ZN
            row = pl.multiple_of(place(block) * BLOCK, BLOCK)
            for half in range(2):
                copies.append(
                    pltpu.make_async_copy(
                        refs[2 * step_y + half].at[pl.ds(step_z * BLOCK, BLOCK), :],
                        scratch.at[pl.ds(row, BLOCK), pl.ds(half * HALF, HALF)],
                        sem.at[len(copies)],
                    )
                )
    return copies


def forward_kernel(*refs):
    x_refs, w_refs = refs[:8], refs[8:16]
    own_ref, down_ref, up_ref = refs[16:19]
    x_scr, w_scr, y_scr, x_sem, w_sem = refs[19:]
    zh, x, c = filt_position()
    copies = []
    for step in range(XN):
        for other in range(CN):
            for far in range(ZH):
                core = c if other == 0 else 1 - c
                high = zh if far == 0 else 1 - zh
                block = filt_index(high, (x + XN - step) % XN, core)
                row = pl.multiple_of(block * BLOCK, BLOCK)
                copies.append(
                    pltpu.make_async_copy(
                        x_refs[2 * step + other].at[pl.ds(far * BLOCK, BLOCK), :],
                        x_scr.at[pl.ds(row, BLOCK), :],
                        x_sem.at[len(copies)],
                    )
                )
    copies += weight_copies(w_refs, w_scr, w_sem, lambda block: block)
    for copy in copies:
        copy.start()
    for copy in copies:
        copy.wait()
    for half in range(2):
        y_scr[half * HALF : (half + 1) * HALF, :] = lax.dot_general(
            w_scr[:, half * HALF : (half + 1) * HALF],
            x_scr[...],
            (((0,), (0,)), ((), ())),
            preferred_element_type=F32,
        )
    cell = lax.broadcasted_iota(jnp.int32, (8, CELLS), 1)
    column = cell % WW
    row_ok = {0: cell >= WW, 2: cell < CELLS - WW}
    col_ok = {0: column >= 1, 2: column < WW - 1}

    def body(part, carry):
        base = pl.multiple_of(part * 8, 8)
        for a, out in ((0, up_ref), (1, own_ref), (2, down_ref)):
            total = None
            for col in range(3):
                lane = None
                for row in range(3):
                    tap = 9 * a + 3 * row + col
                    value = y_scr[pl.ds(tap * BLOCK + base, 8), :]
                    if row != 1:
                        value = pltpu.roll(value, ((1 - row) * WW) % CELLS, 1)
                        value = jnp.where(row_ok[row], value, 0.0)
                    lane = value if lane is None else lane + value
                if col != 1:
                    lane = pltpu.roll(lane, (1 - col) % CELLS, 1)
                    lane = jnp.where(col_ok[col], lane, 0.0)
                total = lane if total is None else total + lane
            out[pl.ds(base, 8), :] = total.astype(out.dtype)
        return carry

    lax.fori_loop(0, BLOCK // 8, body, 0)


def pointwise_kernel(own_ref, below_ref, above_ref, bias_ref, cot_ref, act_ref, grad_ref):
    preact = (
        own_ref[...]
        + below_ref[...].astype(F32)
        + above_ref[...].astype(F32)
        + bias_ref[...].astype(F32)
    )
    sig = jax.nn.sigmoid(preact)
    act_ref[...] = (preact * sig).astype(BF16)
    slope = sig * (1.0 + preact * (1.0 - sig))
    grad_ref[...] = (cot_ref[...].astype(F32) * slope).astype(BF16)


def backward_kernel(*refs):
    grad_refs, w_refs = refs[:3], refs[3:11]
    mine_ref, other_ref = refs[11:13]
    w_scr, g_scr, w_sem = refs[13:]
    zh, x, c = filt_position()

    def place(block):
        high, at, core = block // (XN * CN), (block // CN) % XN, block % CN
        return ((core + c) % CN * XN + (at + XN - x) % XN) * ZH + (high + zh) % ZH

    copies = weight_copies(w_refs, w_scr, w_sem, place)
    for copy in copies:
        copy.start()
    cell = lax.broadcasted_iota(jnp.int32, (16, CELLS), 1)
    column = cell % WW
    row_ok = {2: cell >= WW, 0: cell < CELLS - WW}
    col_ok = {2: column >= 1, 0: column < WW - 1}

    def body(part, carry):
        base = pl.multiple_of(part * 16, 16)
        for a, grad in enumerate(grad_refs):
            plane = grad[pl.ds(base, 16), :].astype(F32)
            for col in range(3):
                lane = plane
                if col != 1:
                    lane = pltpu.roll(lane, (col - 1) % CELLS, 1)
                    lane = jnp.where(col_ok[col], lane, 0.0)
                for row in range(3):
                    value = lane
                    if row != 1:
                        value = pltpu.roll(value, ((row - 1) * WW) % CELLS, 1)
                        value = jnp.where(row_ok[row], value, 0.0)
                    tap = 9 * a + 3 * row + col
                    g_scr[pl.ds(tap * BLOCK + base, 16), :] = value.astype(BF16)
        return carry

    lax.fori_loop(0, BLOCK // 16, body, 0)
    g_scr[TAPS * BLOCK :, :] = jnp.zeros((COLS - TAPS * BLOCK, CELLS), BF16)
    for copy in copies:
        copy.wait()
    half = CHANNELS // 2
    for at, out in ((half, other_ref), (0, mine_ref)):
        out[...] = jnp.dot(
            w_scr[at : at + half, :], g_scr[...], preferred_element_type=F32
        ).astype(BF16)


def shape(rows, columns, dtype=BF16):
    return jax.ShapeDtypeStruct((rows, columns), dtype)


def gather_weights(weights):
    taps_first = jnp.transpose(weights, (1, 0, 2)).reshape(TAPS * BLOCK, BLOCK)
    own = pl.pallas_call(
        transpose_kernel,
        out_shape=shape(BLOCK, COLS),
        in_specs=[VMEM],
        out_specs=VMEM,
        compiler_params=LIMIT,
        name="weights_transpose",
    )(taps_first)
    blocks = [own] + [lax.ppermute(own, "slab", to_z(k)) for k in range(1, ZN)]
    left = jnp.concatenate([block[:, :HALF] for block in blocks], axis=0)
    right = jnp.concatenate([block[:, HALF:] for block in blocks], axis=0)
    left_1 = lax.ppermute(left, "slab", to_y(1))
    right_3 = lax.ppermute(right, "slab", to_y(-1))
    left_3 = lax.ppermute(left, "slab", to_y(-1))
    right_1 = lax.ppermute(right, "slab", to_y(1))
    left_2 = lax.ppermute(left_1, "slab", to_y(1))
    right_2 = lax.ppermute(right_3, "slab", to_y(-1))
    return [left, right, left_1, right_1, left_2, right_2, left_3, right_3]


def gather_inputs(inputs):
    far = lax.ppermute(inputs, "filt", TO_ZHI)
    pair = jnp.concatenate([inputs, far], axis=0)
    pieces = [pair] + [lax.ppermute(pair, "filt", to_x(k)) for k in (1, 2, -1)]
    out = []
    for piece in pieces:
        out += [piece, lax.ppermute(piece, "filt", TO_CORE)]
    return out


def local(inputs, weights, bias, cotangent):
    pieces = gather_inputs(inputs.reshape(BLOCK, CELLS))
    parts = gather_weights(weights)
    own, down, up = pl.pallas_call(
        forward_kernel,
        out_shape=(shape(BLOCK, CELLS, F32), shape(BLOCK, CELLS), shape(BLOCK, CELLS)),
        in_specs=[ANY] * 16,
        out_specs=(VMEM,) * 3,
        scratch_shapes=[
            pltpu.VMEM((CHANNELS, CELLS), BF16),
            pltpu.VMEM((CHANNELS, COLS), BF16),
            pltpu.VMEM((COLS, CELLS), F32),
            pltpu.SemaphoreType.DMA((16,)),
            pltpu.SemaphoreType.DMA((32,)),
        ],
        compiler_params=LIMIT,
        cost_estimate=pl.CostEstimate(
            flops=2 * COLS * CHANNELS * CELLS, bytes_accessed=6 * 2**20, transcendentals=0
        ),
        name="conv_forward",
    )(*pieces, *parts)
    below = lax.ppermute(up, "slab", UP)
    above = lax.ppermute(down, "slab", DOWN)
    activated, grad = pl.pallas_call(
        pointwise_kernel,
        out_shape=(shape(BLOCK, CELLS), shape(BLOCK, CELLS)),
        in_specs=[VMEM] * 5,
        out_specs=(VMEM,) * 2,
        compiler_params=LIMIT,
        name="silu_and_slope",
    )(own, below, above, bias.reshape(BLOCK, 1), cotangent.reshape(BLOCK, CELLS))
    grad_below = lax.ppermute(grad, "slab", UP)
    grad_above = lax.ppermute(grad, "slab", DOWN)
    mine, other = pl.pallas_call(
        backward_kernel,
        out_shape=(shape(CHANNELS // 2, CELLS), shape(CHANNELS // 2, CELLS)),
        in_specs=[VMEM] * 3 + [ANY] * 8,
        out_specs=(VMEM,) * 2,
        scratch_shapes=[
            pltpu.VMEM((CHANNELS, COLS), BF16),
            pltpu.VMEM((COLS, CELLS), BF16),
            pltpu.SemaphoreType.DMA((32,)),
        ],
        compiler_params=LIMIT,
        cost_estimate=pl.CostEstimate(
            flops=2 * COLS * CHANNELS * CELLS, bytes_accessed=6 * 2**20, transcendentals=0
        ),
        name="conv_backward",
    )(grad_above, grad, grad_below, *parts)
    received = lax.ppermute(other, "filt", TO_CORE)
    sums = []
    for k in range(XN):
        rows = slice(k * 2 * BLOCK, (k + 1) * 2 * BLOCK)
        sums.append((mine[rows].astype(F32) + received[rows].astype(F32)).astype(BF16))
    total = sums[0].astype(F32)
    for k in (1, 2, 3):
        total = total + lax.ppermute(sums[k], "filt", to_x(k)).astype(F32)
    far = lax.ppermute(total[BLOCK:].astype(BF16), "filt", TO_ZHI)
    input_grad = (total[:BLOCK] + far.astype(F32)).astype(BF16)
    return activated.reshape(cotangent.shape), input_grad.reshape(inputs.shape)


def solution(mesh):
    return jax.shard_map(
        local,
        mesh=mesh,
        in_specs=(
            P("filt", "slab", None),
            P("filt", None, "slab"),
            P("filt"),
            P("filt", "slab", None),
        ),
        out_specs=(P("filt", "slab", None), P("filt", "slab", None)),
        check_vma=False,
    )
```

```python
import functools

import jax
import jax.numpy as jnp
from jax import lax
from jax.experimental import pallas as pl
from jax.experimental.pallas import tpu as pltpu
from jax.sharding import PartitionSpec as P

HH = 32
WW = 32
CELLS = HH * WW
TAPS = 27
SLOT_TAPS = [*range(9, 18), None, *range(0, 9), *range(18, 27)]
SLOTS = 28
BLOCK = 64
COLS = SLOTS * BLOCK
SAME = 10 * BLOCK
HALF = BLOCK // 2
GROUPS = [(0, 1, 2, 3)]
BLOCKS = 16
CHANNELS = BLOCKS * BLOCK

ZH, XN, CN = 2, 4, 2
YN, ZN = 4, 4

BF16 = jnp.bfloat16
F32 = jnp.float32
LIMIT = pltpu.CompilerParams(vmem_limit_bytes=24 * 1024 * 1024)


def filt_index(zh, x, c):
    return (zh * XN + x) * CN + c


FILT = [(zh, x, c) for zh in range(ZH) for x in range(XN) for c in range(CN)]
SLAB = [(y, z) for y in range(YN) for z in range(ZN)]
TO_CORE = [(filt_index(*d), filt_index(d[0], d[1], 1 - d[2])) for d in FILT]
TO_ZHI = [(filt_index(*d), filt_index(1 - d[0], d[1], d[2])) for d in FILT]


def to_x(k):
    return [(filt_index(*d), filt_index(d[0], (d[1] + k) % XN, d[2])) for d in FILT]


def to_y(k):
    return [(y * ZN + z, ((y + k) % YN) * ZN + z) for y, z in SLAB]


def to_z(k):
    return [(y * ZN + z, y * ZN + (z + k) % ZN) for y, z in SLAB]


UP = [(i, i + 1) for i in range(YN * ZN - 1)]
DOWN = [(i + 1, i) for i in range(YN * ZN - 1)]

VMEM = pl.BlockSpec(memory_space=pltpu.VMEM)
ANY = pl.BlockSpec(memory_space=pl.ANY)
HBM = pl.BlockSpec(memory_space=pltpu.HBM)


def transpose_kernel(w_ref, out_ref):
    for pair in range(0, SLOTS, 2):
        parts = []
        for slot in (pair, pair + 1):
            tap = SLOT_TAPS[slot]
            if tap is None:
                parts.append(jnp.zeros((BLOCK, BLOCK), F32))
            else:
                parts.append(w_ref[tap * BLOCK : (tap + 1) * BLOCK, :].astype(F32))
        turned = jnp.concatenate(parts, axis=0).T
        out_ref[:, pair * BLOCK : (pair + 2) * BLOCK] = turned.astype(BF16)


def filt_position():
    mine = lax.axis_index("filt")
    return mine // (XN * CN), (mine // CN) % XN, mine % CN


def slab_position():
    mine = lax.axis_index("slab")
    return mine // ZN, mine % ZN


def rows_of(block):
    return pl.ds(pl.multiple_of(block * BLOCK, BLOCK), BLOCK)


def weight_copies(pieces, w_scr, sem):
    y, z = slab_position()
    copies = []

    def add(ref, start, row, size):
        place = pl.ds(pl.multiple_of(row, HALF), size)
        copies.append(
            pltpu.make_async_copy(
                ref.at[pl.ds(start, size), :], w_scr.at[place, :], sem.at[len(copies)]
            )
        )

    for at, group in enumerate(GROUPS):
        refs = pieces[5 * at : 5 * at + 5]
        middle = len(group) * HALF
        for step_y in range(YN):
            for index, step_z in enumerate(group):
                block = ((y + YN - step_y) % YN) * ZN + (z + ZN - step_z) % ZN
                row, start = block * BLOCK, index * BLOCK
                if step_y != 2:
                    add(refs[{0: 0, 1: 1, 3: 4}[step_y]], start, row, BLOCK)
                elif start + BLOCK <= middle:
                    add(refs[2], start, row, BLOCK)
                elif start >= middle:
                    add(refs[3], start - middle, row, BLOCK)
                else:
                    add(refs[2], start, row, HALF)
                    add(refs[3], 0, row + HALF, HALF)
    return copies


def input_copies(pieces, x_scr, sem):
    zh, x, c = filt_position()
    copies = []
    for other in range(CN):
        for step in range(XN):
            for far in range(ZH):
                core = c if other == 0 else 1 - c
                high = zh if far == 0 else 1 - zh
                block = filt_index(high, (x + XN - step) % XN, core)
                copies.append(
                    pltpu.make_async_copy(
                        pieces[other].at[pl.ds((step * ZH + far) * BLOCK, BLOCK), :],
                        x_scr.at[rows_of(block), :],
                        sem.at[len(copies)],
                    )
                )
    return copies


def start_all(copies):
    for copy in copies:
        copy.start()


def wait_all(copies):
    for copy in copies:
        copy.wait()


def shifted_sum(y_scr, first, base):
    cell = lax.broadcasted_iota(jnp.int32, (8, CELLS), 1)
    column = cell % WW
    row_ok = {0: cell >= WW, 2: cell < CELLS - WW}
    col_ok = {0: column >= 1, 2: column < WW - 1}
    total = None
    for col in range(3):
        lane = None
        for row in range(3):
            value = y_scr[pl.ds((first + 3 * row + col) * BLOCK + base, 8), :]
            if row != 1:
                value = pltpu.roll(value, ((1 - row) * WW) % CELLS, 1)
                value = jnp.where(row_ok[row], value, 0.0)
            lane = value if lane is None else lane + value
        if col != 1:
            lane = pltpu.roll(lane, (1 - col) % CELLS, 1)
            lane = jnp.where(col_ok[col], lane, 0.0)
        total = lane if total is None else total + lane
    return total


def convolve(planes, w, x, out_refs, y_scr):
    y_scr[...] = lax.dot_general(w, x, (((0,), (0,)), ((), ())), preferred_element_type=F32)

    def body(part, carry):
        base = pl.multiple_of(part * 8, 8)
        for first, out in zip(planes, out_refs):
            out[pl.ds(base, 8), :] = shifted_sum(y_scr, first, base).astype(out.dtype)
        return carry

    lax.fori_loop(0, BLOCK // 8, body, 0)


def forward_beside_kernel(*refs):
    count = 2 + 5 * len(GROUPS)
    x_pieces, w_pieces = refs[:2], refs[2:count]
    matrix_ref, up_ref, down_ref = refs[count + 1 : count + 4]
    x_scr, w_scr, y_scr, x_sem, w_sem, out_sem = refs[count + 4 :]
    copies = input_copies(x_pieces, x_scr, x_sem) + weight_copies(w_pieces, w_scr, w_sem)
    start_all(copies)
    wait_all(copies)
    keep = pltpu.make_async_copy(w_scr, matrix_ref, out_sem)
    keep.start()
    convolve((0, 9), w_scr[:, SAME:], x_scr[...], (up_ref, down_ref), y_scr)
    keep.wait()


def ready_kernel(*refs):
    refs[-1][...] = jnp.zeros((8, 128), BF16)


def forward_same_kernel(*refs):
    x_pieces, matrix_ref, own_ref = refs[:2], refs[2], refs[3]
    x_scr, w_scr, y_scr, x_sem, w_sem = refs[4:]
    copies = input_copies(x_pieces, x_scr, x_sem)
    copies.append(pltpu.make_async_copy(matrix_ref.at[:, pl.ds(0, SAME)], w_scr, w_sem))
    start_all(copies)
    wait_all(copies)
    convolve((0,), w_scr[...], x_scr[...], (own_ref,), y_scr)


def pointwise_kernel(own_ref, below_ref, above_ref, bias_ref, cot_ref, act_ref, grad_ref):
    preact = (
        own_ref[...]
        + below_ref[...].astype(F32)
        + above_ref[...].astype(F32)
        + bias_ref[...].astype(F32)
    )
    sig = jax.nn.sigmoid(preact)
    act_ref[...] = (preact * sig).astype(BF16)
    slope = sig * (1.0 + preact * (1.0 - sig))
    grad_ref[...] = (cot_ref[...].astype(F32) * slope).astype(BF16)


def stack_taps(grad_refs, g_scr):
    cell = lax.broadcasted_iota(jnp.int32, (16, CELLS), 1)
    column = cell % WW
    row_ok = {2: cell >= WW, 0: cell < CELLS - WW}
    col_ok = {2: column >= 1, 0: column < WW - 1}

    def body(part, carry):
        base = pl.multiple_of(part * 16, 16)
        for at, grad in enumerate(grad_refs):
            plane = grad[pl.ds(base, 16), :].astype(F32)
            for col in range(3):
                lane = plane
                if col != 1:
                    lane = pltpu.roll(lane, (col - 1) % CELLS, 1)
                    lane = jnp.where(col_ok[col], lane, 0.0)
                for row in range(3):
                    value = lane
                    if row != 1:
                        value = pltpu.roll(value, ((row - 1) * WW) % CELLS, 1)
                        value = jnp.where(row_ok[row], value, 0.0)
                    slot = 9 * at + 3 * row + col
                    g_scr[pl.ds(slot * BLOCK + base, 16), :] = value.astype(BF16)
        return carry

    lax.fori_loop(0, BLOCK // 16, body, 0)


def backward_same_kernel(grad_ref, matrix_ref, out_ref, w_scr, g_scr, sem):
    copy = pltpu.make_async_copy(matrix_ref.at[:, pl.ds(0, SAME)], w_scr, sem)
    copy.start()
    stack_taps([grad_ref], g_scr)
    g_scr[9 * BLOCK :, :] = jnp.zeros((BLOCK, CELLS), BF16)
    copy.wait()
    half = CHANNELS // 2
    for start in (0, half):
        out_ref[start : start + half, :] = jnp.dot(
            w_scr[start : start + half, :], g_scr[...], preferred_element_type=F32
        )


def backward_beside_kernel(far, *refs):
    above_ref, below_ref, same_ref, matrix_ref, out_ref, w_scr, g_scr, sem = refs
    zh, x, c = filt_position()
    size = CHANNELS // 2
    first = pl.multiple_of(((zh + far) % ZH) * size, size)
    copy = pltpu.make_async_copy(
        matrix_ref.at[pl.ds(first, size), pl.ds(SAME, COLS - SAME)], w_scr, sem
    )
    copy.start()
    stack_taps([above_ref, below_ref], g_scr)
    copy.wait()
    total = same_ref[pl.ds(first, size), :] + jnp.dot(
        w_scr[...], g_scr[...], preferred_element_type=F32
    )
    total = total.astype(BF16)
    for at in range(size // BLOCK):
        along, core = at // CN, at % CN
        place = (core + c) % CN * XN + (along + XN - x) % XN
        out_ref[rows_of(place), :] = total[at * BLOCK : (at + 1) * BLOCK, :]


def shape(rows, columns, dtype=BF16):
    return jax.ShapeDtypeStruct((rows, columns), dtype)


def call(kernel, name, outs, scratch, columns, operands, in_any=(), in_hbm=(), out_hbm=(), limit=None):
    cost = None
    if columns:
        cost = pl.CostEstimate(
            flops=2 * columns * CHANNELS * CELLS, bytes_accessed=2**20, transcendentals=0
        )
    return pl.pallas_call(
        kernel,
        out_shape=outs,
        in_specs=[
            ANY if at in in_any else HBM if at in in_hbm else VMEM for at in range(len(operands))
        ],
        out_specs=tuple(HBM if at in out_hbm else VMEM for at in range(len(outs))),
        scratch_shapes=scratch,
        compiler_params=pltpu.CompilerParams(vmem_limit_bytes=(limit or 24) * 2**20),
        cost_estimate=cost,
        name=name,
    )(*operands)


def gather_weights(weights):
    taps_first = jnp.transpose(weights, (1, 0, 2)).reshape(TAPS * BLOCK, BLOCK)
    (own,) = call(
        transpose_kernel, "weights_transpose", (shape(BLOCK, COLS),), [], 0, [taps_first]
    )
    blocks = [own] + [lax.ppermute(own, "slab", to_z(k)) for k in range(1, ZN)]
    pieces = []
    for group in GROUPS:
        line = jnp.concatenate([blocks[k] for k in group], axis=0)
        half = line.shape[0] // 2
        before = lax.ppermute(line, "slab", to_y(1))
        after = lax.ppermute(line, "slab", to_y(-1))
        first = lax.ppermute(before[:half], "slab", to_y(1))
        second = lax.ppermute(after[half:], "slab", to_y(-1))
        pieces += [line, before, first, second, after]
    return pieces


def gather_inputs(inputs, w_pieces):
    far = lax.ppermute(lax.optimization_barrier((inputs, w_pieces[0]))[0], "filt", TO_ZHI)
    pair = jnp.concatenate([inputs, far], axis=0)
    row = jnp.concatenate(
        [pair] + [lax.ppermute(pair, "filt", to_x(k)) for k in range(1, XN)], axis=0
    )
    return [row, lax.ppermute(row, "filt", TO_CORE)]


def sum_over_row(part):
    size = part.shape[0] // 2
    received = lax.ppermute(part[size:], "filt", TO_CORE)
    sums = []
    for k in range(XN):
        rows = slice(k * BLOCK, (k + 1) * BLOCK)
        sums.append((part[rows].astype(F32) + received[rows].astype(F32)).astype(BF16))
    arrived = [lax.ppermute(sums[k], "filt", to_x(k)) for k in range(1, XN)]
    result = sums[0].astype(F32)
    for piece in arrived:
        result = result + piece.astype(F32)
    return result


def local(inputs, weights, bias, cotangent):
    w_pieces = gather_weights(weights)
    x_pieces = gather_inputs(inputs.reshape(BLOCK, CELLS), w_pieces)
    (ready,) = call(
        ready_kernel, "weights_ready", (shape(8, 128),), [], 7168, w_pieces[2:4], in_any=range(2)
    )
    x_scratch = pltpu.VMEM((CHANNELS, CELLS), BF16)
    matrix, up, down = call(
        forward_beside_kernel,
        "forward_beside",
        (shape(CHANNELS, COLS), shape(BLOCK, CELLS), shape(BLOCK, CELLS)),
        [
            x_scratch,
            pltpu.VMEM((CHANNELS, COLS), BF16),
            pltpu.VMEM((COLS - SAME, CELLS), F32),
            pltpu.SemaphoreType.DMA((BLOCKS,)),
            pltpu.SemaphoreType.DMA((2 * BLOCKS,)),
            pltpu.SemaphoreType.DMA,
        ],
        COLS - SAME,
        x_pieces + w_pieces + [ready],
        in_any=range(3 + len(w_pieces)),
        out_hbm=(0,),
        limit=56,
    )
    below = lax.ppermute(up, "slab", UP)
    above = lax.ppermute(down, "slab", DOWN)
    (own,) = call(
        forward_same_kernel,
        "forward_same",
        (shape(BLOCK, CELLS, F32),),
        [
            x_scratch,
            pltpu.VMEM((CHANNELS, SAME), BF16),
            pltpu.VMEM((SAME, CELLS), F32),
            pltpu.SemaphoreType.DMA((BLOCKS,)),
            pltpu.SemaphoreType.DMA,
        ],
        SAME,
        x_pieces + [matrix],
        in_any=range(2),
        in_hbm=(2,),
        limit=55,
    )
    activated, grad = call(
        pointwise_kernel,
        "silu_and_slope",
        (shape(BLOCK, CELLS), shape(BLOCK, CELLS)),
        [],
        0,
        [own, below, above, bias.reshape(BLOCK, 1), cotangent.reshape(BLOCK, CELLS)],
    )
    grad_below = lax.ppermute(grad, "slab", UP)
    grad_above = lax.ppermute(grad, "slab", DOWN)
    (same,) = call(
        backward_same_kernel,
        "backward_same",
        (shape(CHANNELS, CELLS, F32),),
        [
            pltpu.VMEM((CHANNELS, SAME), BF16),
            pltpu.VMEM((SAME, CELLS), BF16),
            pltpu.SemaphoreType.DMA,
        ],
        SAME,
        [grad, matrix],
        in_hbm=(1,),
    )
    sums = []
    for far, name in ((1, "backward_far"), (0, "backward_near")):
        (part,) = call(
            functools.partial(backward_beside_kernel, far),
            name,
            (shape(CHANNELS // 2, CELLS),),
            [
                pltpu.VMEM((CHANNELS // 2, COLS - SAME), BF16),
                pltpu.VMEM((COLS - SAME, CELLS), BF16),
                pltpu.SemaphoreType.DMA,
            ],
            (COLS - SAME) // 2,
            [grad_above, grad_below, same, matrix],
            in_hbm=(3,),
        )
        sums.append(sum_over_row(part))
    arrived = lax.ppermute(sums[0].astype(BF16), "filt", TO_ZHI)
    input_grad = (sums[1] + arrived.astype(F32)).astype(BF16)
    return activated.reshape(cotangent.shape), input_grad.reshape(inputs.shape)


def solution(mesh):
    return jax.shard_map(
        local,
        mesh=mesh,
        in_specs=(
            P("filt", "slab", None),
            P("filt", None, "slab"),
            P("filt"),
            P("filt", "slab", None),
        ),
        out_specs=(P("filt", "slab", None), P("filt", "slab", None)),
        check_vma=False,
    )
```

```python
import functools

import jax
import jax.numpy as jnp
from jax import lax
from jax.experimental import pallas as pl
from jax.experimental.pallas import tpu as pltpu
from jax.sharding import PartitionSpec as P

HH = 32
WW = 32
CELLS = HH * WW
TAPS = 27
SLOT_TAPS = [*range(9, 18), None, *range(0, 9), *range(18, 27)]
SLOTS = 28
BLOCK = 64
COLS = SLOTS * BLOCK
SAME = 10 * BLOCK
BESIDE = COLS - SAME
BLOCKS = 16
CHANNELS = BLOCKS * BLOCK

ZH, XN, CN = 2, 4, 2
YN, ZN = 4, 4

BF16 = jnp.bfloat16
F32 = jnp.float32


def filt_index(zh, x, c):
    return (zh * XN + x) * CN + c


FILT = [(zh, x, c) for zh in range(ZH) for x in range(XN) for c in range(CN)]
SLAB = [(y, z) for y in range(YN) for z in range(ZN)]
TO_CORE = [(filt_index(*d), filt_index(d[0], d[1], 1 - d[2])) for d in FILT]
TO_ZHI = [(filt_index(*d), filt_index(1 - d[0], d[1], d[2])) for d in FILT]


def to_x(k):
    return [(filt_index(*d), filt_index(d[0], (d[1] + k) % XN, d[2])) for d in FILT]


def to_y(k):
    return [(y * ZN + z, ((y + k) % YN) * ZN + z) for y, z in SLAB]


def to_z(k):
    return [(y * ZN + z, y * ZN + (z + k) % ZN) for y, z in SLAB]


UP = [(i, i + 1) for i in range(YN * ZN - 1)]
DOWN = [(i + 1, i) for i in range(YN * ZN - 1)]

VMEM = pl.BlockSpec(memory_space=pltpu.VMEM)
ANY = pl.BlockSpec(memory_space=pl.ANY)


def transpose_kernel(w_ref, out_ref):
    for pair in range(0, SLOTS, 2):
        parts = []
        for slot in (pair, pair + 1):
            tap = SLOT_TAPS[slot]
            if tap is None:
                parts.append(jnp.zeros((BLOCK, BLOCK), F32))
            else:
                parts.append(w_ref[tap * BLOCK : (tap + 1) * BLOCK, :].astype(F32))
        turned = jnp.concatenate(parts, axis=0).T
        out_ref[:, pair * BLOCK : (pair + 2) * BLOCK] = turned.astype(BF16)


def filt_position():
    mine = lax.axis_index("filt")
    return mine // (XN * CN), (mine // CN) % XN, mine % CN


def slab_position():
    mine = lax.axis_index("slab")
    return mine // ZN, mine % ZN


def rows_of(block):
    return pl.ds(pl.multiple_of(block * BLOCK, BLOCK), BLOCK)


def assemble_weights(pieces, same_ref, beside_ref):
    y, z = slab_position()
    half = BLOCK // 2
    for step_y in range(YN):
        for step_z in range(ZN):
            group, index = (0, 0) if step_z == 0 else (5, step_z - 1)
            block = ((y + YN - step_y) % YN) * ZN + (z + ZN - step_z) % ZN
            for part in range(2):
                start = index * BLOCK + part * half
                if step_y == 2:
                    middle = half if step_z == 0 else 3 * half
                    ref = pieces[group + (2 if start < middle else 3)]
                    start %= middle
                else:
                    ref = pieces[group + {0: 0, 1: 1, 3: 4}[step_y]]
                rows = pl.ds(pl.multiple_of(block * BLOCK + part * half, half), half)
                same_ref[rows, :] = ref[start : start + half, :SAME]
                beside_ref[rows, :] = ref[start : start + half, SAME:]


def assemble_inputs(pieces, x_ref):
    zh, x, c = filt_position()
    for other in range(CN):
        for step in range(XN):
            for far in range(ZH):
                core = c if other == 0 else 1 - c
                high = zh if far == 0 else 1 - zh
                block = filt_index(high, (x + XN - step) % XN, core)
                start = (step * ZH + far) * BLOCK
                x_ref[rows_of(block), :] = pieces[other][start : start + BLOCK, :]


def shifted_sum(y_scr, first, base):
    cell = lax.broadcasted_iota(jnp.int32, (8, CELLS), 1)
    column = cell % WW
    row_ok = {0: cell >= WW, 2: cell < CELLS - WW}
    col_ok = {0: column >= 1, 2: column < WW - 1}
    total = None
    for col in range(3):
        lane = None
        for row in range(3):
            value = y_scr[pl.ds((first + 3 * row + col) * BLOCK + base, 8), :]
            if row != 1:
                value = pltpu.roll(value, ((1 - row) * WW) % CELLS, 1)
                value = jnp.where(row_ok[row], value, 0.0)
            lane = value if lane is None else lane + value
        if col != 1:
            lane = pltpu.roll(lane, (1 - col) % CELLS, 1)
            lane = jnp.where(col_ok[col], lane, 0.0)
        total = lane if total is None else total + lane
    return total


def convolve(planes, w, x, out_refs, y_scr):
    y_scr[...] = lax.dot_general(w, x, (((0,), (0,)), ((), ())), preferred_element_type=F32)

    def body(part, carry):
        base = pl.multiple_of(part * 8, 8)
        for first, out in zip(planes, out_refs):
            out[pl.ds(base, 8), :] = shifted_sum(y_scr, first, base).astype(out.dtype)
        return carry

    lax.fori_loop(0, BLOCK // 8, body, 0)


def forward_beside_kernel(*refs):
    x_pieces, w_pieces = refs[:2], refs[2:12]
    x_ref, same_ref, beside_ref, up_ref, down_ref, w_scr, y_scr, sem = refs[13:]
    assemble_inputs(x_pieces, x_ref)
    assemble_weights(w_pieces, same_ref, w_scr)
    keep = pltpu.make_async_copy(w_scr, beside_ref, sem)
    keep.start()
    convolve((0, 9), w_scr[...], x_ref[...], (up_ref, down_ref), y_scr)
    keep.wait()


def ready_kernel(*refs):
    refs[-1][...] = jnp.zeros((8, 128), BF16)


def forward_same_kernel(x_ref, same_ref, own_ref, y_scr):
    convolve((0,), same_ref[...], x_ref[...], (own_ref,), y_scr)


def pointwise_kernel(own_ref, below_ref, above_ref, bias_ref, cot_ref, act_ref, grad_ref):
    preact = (
        own_ref[...]
        + below_ref[...].astype(F32)
        + above_ref[...].astype(F32)
        + bias_ref[...].astype(F32)
    )
    sig = jax.nn.sigmoid(preact)
    act_ref[...] = (preact * sig).astype(BF16)
    slope = sig * (1.0 + preact * (1.0 - sig))
    grad_ref[...] = (cot_ref[...].astype(F32) * slope).astype(BF16)


def stack_taps(grad_refs, g_scr):
    cell = lax.broadcasted_iota(jnp.int32, (16, CELLS), 1)
    column = cell % WW
    row_ok = {2: cell >= WW, 0: cell < CELLS - WW}
    col_ok = {2: column >= 1, 0: column < WW - 1}

    def body(part, carry):
        base = pl.multiple_of(part * 16, 16)
        for at, grad in enumerate(grad_refs):
            plane = grad[pl.ds(base, 16), :].astype(F32)
            for col in range(3):
                lane = plane
                if col != 1:
                    lane = pltpu.roll(lane, (col - 1) % CELLS, 1)
                    lane = jnp.where(col_ok[col], lane, 0.0)
                for row in range(3):
                    value = lane
                    if row != 1:
                        value = pltpu.roll(value, ((row - 1) * WW) % CELLS, 1)
                        value = jnp.where(row_ok[row], value, 0.0)
                    slot = 9 * at + 3 * row + col
                    g_scr[pl.ds(slot * BLOCK + base, 16), :] = value.astype(BF16)
        return carry

    lax.fori_loop(0, BLOCK // 16, body, 0)


def backward_same_kernel(grad_ref, w_ref, out_ref, g_scr):
    stack_taps([grad_ref], g_scr)
    g_scr[9 * BLOCK :, :] = jnp.zeros((BLOCK, CELLS), BF16)
    half = CHANNELS // 2
    for start in (0, half):
        out_ref[start : start + half, :] = jnp.dot(
            w_ref[start : start + half, :], g_scr[...], preferred_element_type=F32
        )


def backward_beside_kernel(far, above_ref, below_ref, same_ref, w_ref, out_ref, g_scr):
    zh, x, c = filt_position()
    size = CHANNELS // 2
    first = pl.multiple_of(((zh + far) % ZH) * size, size)
    stack_taps([above_ref, below_ref], g_scr)
    total = same_ref[pl.ds(first, size), :] + jnp.dot(
        w_ref[pl.ds(first, size), :], g_scr[...], preferred_element_type=F32
    )
    total = total.astype(BF16)
    for at in range(size // BLOCK):
        along, core = at // CN, at % CN
        place = (core + c) % CN * XN + (along + XN - x) % XN
        out_ref[rows_of(place), :] = total[at * BLOCK : (at + 1) * BLOCK, :]


def shape(rows, columns, dtype=BF16):
    return jax.ShapeDtypeStruct((rows, columns), dtype)


def call(kernel, name, outs, scratch, columns, operands, in_any=(), out_any=(), limit=24):
    cost = None
    if columns:
        cost = pl.CostEstimate(
            flops=2 * columns * CHANNELS * CELLS, bytes_accessed=2**20, transcendentals=0
        )
    return pl.pallas_call(
        kernel,
        out_shape=outs,
        in_specs=[ANY if at in in_any else VMEM for at in range(len(operands))],
        out_specs=tuple(ANY if at in out_any else VMEM for at in range(len(outs))),
        scratch_shapes=scratch,
        compiler_params=pltpu.CompilerParams(vmem_limit_bytes=limit * 2**20),
        cost_estimate=cost,
        name=name,
    )(*operands)


def gather_weights(weights):
    taps_first = jnp.transpose(weights, (1, 0, 2)).reshape(TAPS * BLOCK, BLOCK)
    (own,) = call(
        transpose_kernel, "weights_transpose", (shape(BLOCK, COLS),), [], 0, [taps_first]
    )
    beside = [lax.ppermute(own, "slab", to_z(k)) for k in range(1, ZN)]
    pieces = along_y(own)
    line = jnp.concatenate(beside, axis=0)
    return pieces + along_y(once(line, pieces[2], pieces[3]))


def once(value, *others):
    return lax.optimization_barrier((value, *others))[0]


def along_y(line):
    half = line.shape[0] // 2
    before = lax.ppermute(line, "slab", to_y(1))
    after = lax.ppermute(line, "slab", to_y(-1))
    first = lax.ppermute(before[:half], "slab", to_y(1))
    second = lax.ppermute(after[half:], "slab", to_y(-1))
    return [line, before, first, second, after]


def gather_inputs(inputs, w_pieces):
    far = lax.ppermute(once(inputs, w_pieces[5]), "filt", TO_ZHI)
    pair = jnp.concatenate([inputs, far], axis=0)
    row = jnp.concatenate(
        [pair] + [lax.ppermute(pair, "filt", to_x(k)) for k in range(1, XN)], axis=0
    )
    return [row, lax.ppermute(row, "filt", TO_CORE)]


def sum_over_row(part):
    size = part.shape[0] // 2
    received = lax.ppermute(part[size:], "filt", TO_CORE)
    sums = []
    for k in range(XN):
        rows = slice(k * BLOCK, (k + 1) * BLOCK)
        sums.append((part[rows].astype(F32) + received[rows].astype(F32)).astype(BF16))
    arrived = [lax.ppermute(sums[k], "filt", to_x(k)) for k in range(1, XN)]
    result = sums[0].astype(F32)
    for piece in arrived:
        result = result + piece.astype(F32)
    return result


def local(inputs, weights, bias, cotangent):
    w_pieces = gather_weights(weights)
    x_pieces = gather_inputs(inputs.reshape(BLOCK, CELLS), w_pieces)
    (ready,) = call(
        ready_kernel, "weights_ready", (shape(8, 128),), [], 7168, w_pieces[7:9], in_any=range(2)
    )
    channels, same_taps, beside_taps, up, down = call(
        forward_beside_kernel,
        "forward_beside",
        (
            shape(CHANNELS, CELLS),
            shape(CHANNELS, SAME),
            shape(CHANNELS, BESIDE),
            shape(BLOCK, CELLS),
            shape(BLOCK, CELLS),
        ),
        [
            pltpu.VMEM((CHANNELS, BESIDE), BF16),
            pltpu.VMEM((BESIDE, CELLS), F32),
            pltpu.SemaphoreType.DMA,
        ],
        BESIDE,
        x_pieces + w_pieces + [ready],
        in_any=(12,),
        out_any=(2,),
        limit=46,
    )
    below = lax.ppermute(up, "slab", UP)
    above = lax.ppermute(down, "slab", DOWN)
    (own,) = call(
        forward_same_kernel,
        "forward_same",
        (shape(BLOCK, CELLS, F32),),
        [pltpu.VMEM((SAME, CELLS), F32)],
        SAME,
        [channels, same_taps],
    )
    activated, grad = call(
        pointwise_kernel,
        "silu_and_slope",
        (shape(BLOCK, CELLS), shape(BLOCK, CELLS)),
        [],
        0,
        [own, below, above, bias.reshape(BLOCK, 1), cotangent.reshape(BLOCK, CELLS)],
    )
    grad_below = lax.ppermute(grad, "slab", UP)
    grad_above = lax.ppermute(grad, "slab", DOWN)
    (same,) = call(
        backward_same_kernel,
        "backward_same",
        (shape(CHANNELS, CELLS, F32),),
        [pltpu.VMEM((SAME, CELLS), BF16)],
        SAME,
        [grad, same_taps],
    )
    sums = []
    for far, name in ((1, "backward_far"), (0, "backward_near")):
        (part,) = call(
            functools.partial(backward_beside_kernel, far),
            name,
            (shape(CHANNELS // 2, CELLS),),
            [pltpu.VMEM((BESIDE, CELLS), BF16)],
            BESIDE // 2,
            [grad_above, grad_below, same, beside_taps],
        )
        sums.append(sum_over_row(part))
    arrived = lax.ppermute(sums[0].astype(BF16), "filt", TO_ZHI)
    input_grad = (sums[1] + arrived.astype(F32)).astype(BF16)
    return activated.reshape(cotangent.shape), input_grad.reshape(inputs.shape)


def solution(mesh):
    return jax.shard_map(
        local,
        mesh=mesh,
        in_specs=(
            P("filt", "slab", None),
            P("filt", None, "slab"),
            P("filt"),
            P("filt", "slab", None),
        ),
        out_specs=(P("filt", "slab", None), P("filt", "slab", None)),
        check_vma=False,
    )
```

```python
import jax
import jax.numpy as jnp
from jax import lax
from jax.experimental import pallas as pl
from jax.experimental.pallas import tpu as pltpu
from jax.sharding import PartitionSpec as P

HH = 32
WW = 32
CELLS = HH * WW
TAPS = 27
SLOT_TAPS = [*range(9, 18), None, *range(0, 9), *range(18, 27)]
SLOTS = 28
BLOCK = 64
COLS = SLOTS * BLOCK
SAME = 10 * BLOCK
BESIDE = COLS - SAME
BLOCKS = 16
CHANNELS = BLOCKS * BLOCK

ZH, XN, CN = 2, 4, 2
YN, ZN = 4, 4

BF16 = jnp.bfloat16
F32 = jnp.float32


def filt_index(zh, x, c):
    return (zh * XN + x) * CN + c


FILT = [(zh, x, c) for zh in range(ZH) for x in range(XN) for c in range(CN)]
SLAB = [(y, z) for y in range(YN) for z in range(ZN)]
TO_CORE = [(filt_index(*d), filt_index(d[0], d[1], 1 - d[2])) for d in FILT]
TO_ZHI = [(filt_index(*d), filt_index(1 - d[0], d[1], d[2])) for d in FILT]


def to_x(k):
    return [(filt_index(*d), filt_index(d[0], (d[1] + k) % XN, d[2])) for d in FILT]


def to_y(k):
    return [(y * ZN + z, ((y + k) % YN) * ZN + z) for y, z in SLAB]


def to_z(k):
    return [(y * ZN + z, y * ZN + (z + k) % ZN) for y, z in SLAB]


UP = [(i, i + 1) for i in range(YN * ZN - 1)]
DOWN = [(i + 1, i) for i in range(YN * ZN - 1)]

VMEM = pl.BlockSpec(memory_space=pltpu.VMEM)
ANY = pl.BlockSpec(memory_space=pl.ANY)


def transpose_kernel(w_ref, out_ref):
    for pair in range(0, SLOTS, 2):
        parts = []
        for slot in (pair, pair + 1):
            tap = SLOT_TAPS[slot]
            if tap is None:
                parts.append(jnp.zeros((BLOCK, BLOCK), F32))
            else:
                parts.append(w_ref[tap * BLOCK : (tap + 1) * BLOCK, :].astype(F32))
        turned = jnp.concatenate(parts, axis=0).T
        out_ref[:, pair * BLOCK : (pair + 2) * BLOCK] = turned.astype(BF16)


def filt_position():
    mine = lax.axis_index("filt")
    return mine // (XN * CN), (mine // CN) % XN, mine % CN


def slab_position():
    mine = lax.axis_index("slab")
    return mine // ZN, mine % ZN


def rows_of(block):
    return pl.ds(pl.multiple_of(block * BLOCK, BLOCK), BLOCK)


def assemble_weights(pieces, same_ref, beside_ref):
    y, z = slab_position()
    half = BLOCK // 2
    for step_y in range(YN):
        for step_z in range(ZN):
            group, index = (0, 0) if step_z == 0 else (5, step_z - 1)
            block = ((y + YN - step_y) % YN) * ZN + (z + ZN - step_z) % ZN
            for part in range(2):
                start = index * BLOCK + part * half
                if step_y == 2:
                    middle = half if step_z == 0 else 3 * half
                    ref = pieces[group + (2 if start < middle else 3)]
                    start %= middle
                else:
                    ref = pieces[group + {0: 0, 1: 1, 3: 4}[step_y]]
                rows = pl.ds(pl.multiple_of(block * BLOCK + part * half, half), half)
                same_ref[rows, :] = ref[start : start + half, :SAME]
                beside_ref[rows, :] = ref[start : start + half, SAME:]


def assemble_inputs(pieces, x_ref):
    zh, x, c = filt_position()
    for other in range(CN):
        for step in range(XN):
            for far in range(ZH):
                core = c if other == 0 else 1 - c
                high = zh if far == 0 else 1 - zh
                block = filt_index(high, (x + XN - step) % XN, core)
                start = (step * ZH + far) * BLOCK
                x_ref[rows_of(block), :] = pieces[other][start : start + BLOCK, :]


def shifted_sum(y_scr, first, base):
    cell = lax.broadcasted_iota(jnp.int32, (8, CELLS), 1)
    column = cell % WW
    row_ok = {0: cell >= WW, 2: cell < CELLS - WW}
    col_ok = {0: column >= 1, 2: column < WW - 1}
    total = None
    for col in range(3):
        lane = None
        for row in range(3):
            value = y_scr[pl.ds((first + 3 * row + col) * BLOCK + base, 8), :]
            if row != 1:
                value = pltpu.roll(value, ((1 - row) * WW) % CELLS, 1)
                value = jnp.where(row_ok[row], value, 0.0)
            lane = value if lane is None else lane + value
        if col != 1:
            lane = pltpu.roll(lane, (1 - col) % CELLS, 1)
            lane = jnp.where(col_ok[col], lane, 0.0)
        total = lane if total is None else total + lane
    return total


def convolve(planes, w, x, out_refs, y_scr):
    y_scr[...] = lax.dot_general(w, x, (((0,), (0,)), ((), ())), preferred_element_type=F32)

    def body(part, carry):
        base = pl.multiple_of(part * 8, 8)
        for first, out in zip(planes, out_refs):
            out[pl.ds(base, 8), :] = shifted_sum(y_scr, first, base).astype(out.dtype)
        return carry

    lax.fori_loop(0, BLOCK // 8, body, 0)


def forward_beside_kernel(*refs):
    x_pieces, w_pieces = refs[:2], refs[2:12]
    same_ref, beside_ref, up_ref, down_ref, x_scr, w_scr, y_scr, sem = refs[13:]
    assemble_inputs(x_pieces, x_scr)
    assemble_weights(w_pieces, same_ref, w_scr)
    keep = pltpu.make_async_copy(w_scr, beside_ref, sem)
    keep.start()
    convolve((0, 9), w_scr[...], x_scr[...], (up_ref, down_ref), y_scr)
    keep.wait()


def ready_kernel(*refs):
    refs[-1][...] = jnp.zeros((8, 128), BF16)


def forward_same_kernel(first_ref, second_ref, same_ref, own_ref, x_scr, y_scr):
    assemble_inputs((first_ref, second_ref), x_scr)
    convolve((0,), same_ref[...], x_scr[...], (own_ref,), y_scr)


def pointwise_kernel(own_ref, below_ref, above_ref, bias_ref, cot_ref, act_ref, grad_ref):
    preact = (
        own_ref[...]
        + below_ref[...].astype(F32)
        + above_ref[...].astype(F32)
        + bias_ref[...].astype(F32)
    )
    sig = jax.nn.sigmoid(preact)
    act_ref[...] = (preact * sig).astype(BF16)
    slope = sig * (1.0 + preact * (1.0 - sig))
    grad_ref[...] = (cot_ref[...].astype(F32) * slope).astype(BF16)


def stack_taps(grad_refs, g_scr):
    cell = lax.broadcasted_iota(jnp.int32, (16, CELLS), 1)
    column = cell % WW
    row_ok = {2: cell >= WW, 0: cell < CELLS - WW}
    col_ok = {2: column >= 1, 0: column < WW - 1}

    def body(part, carry):
        base = pl.multiple_of(part * 16, 16)
        for at, grad in enumerate(grad_refs):
            plane = grad[pl.ds(base, 16), :].astype(F32)
            for col in range(3):
                lane = plane
                if col != 1:
                    lane = pltpu.roll(lane, (col - 1) % CELLS, 1)
                    lane = jnp.where(col_ok[col], lane, 0.0)
                for row in range(3):
                    value = lane
                    if row != 1:
                        value = pltpu.roll(value, ((row - 1) * WW) % CELLS, 1)
                        value = jnp.where(row_ok[row], value, 0.0)
                    slot = 9 * at + 3 * row + col
                    g_scr[pl.ds(slot * BLOCK + base, 16), :] = value.astype(BF16)
        return carry

    lax.fori_loop(0, BLOCK // 16, body, 0)


def backward_same_kernel(grad_ref, w_ref, out_ref, g_scr):
    stack_taps([grad_ref], g_scr)
    g_scr[9 * BLOCK :, :] = jnp.zeros((BLOCK, CELLS), BF16)
    half = CHANNELS // 2
    for start in (0, half):
        out_ref[start : start + half, :] = jnp.dot(
            w_ref[start : start + half, :], g_scr[...], preferred_element_type=F32
        )


def backward_far_kernel(above_ref, below_ref, same_ref, w_ref, out_ref, g_ref):
    stack_taps([above_ref, below_ref], g_ref)
    backward_rows(1, g_ref, same_ref, w_ref, out_ref)


def backward_near_kernel(g_ref, same_ref, w_ref, out_ref):
    backward_rows(0, g_ref, same_ref, w_ref, out_ref)


def backward_rows(far, g_ref, same_ref, w_ref, out_ref):
    zh, x, c = filt_position()
    size = CHANNELS // 2
    first = pl.multiple_of(((zh + far) % ZH) * size, size)
    total = same_ref[pl.ds(first, size), :] + jnp.dot(
        w_ref[pl.ds(first, size), :], g_ref[...], preferred_element_type=F32
    )
    total = total.astype(BF16)
    for at in range(size // BLOCK):
        along, core = at // CN, at % CN
        place = (core + c) % CN * XN + (along + XN - x) % XN
        out_ref[rows_of(place), :] = total[at * BLOCK : (at + 1) * BLOCK, :]


def shape(rows, columns, dtype=BF16):
    return jax.ShapeDtypeStruct((rows, columns), dtype)


def call(kernel, name, outs, scratch, columns, operands, in_any=(), out_any=(), limit=24):
    cost = None
    if columns:
        cost = pl.CostEstimate(
            flops=2 * columns * CHANNELS * CELLS, bytes_accessed=2**20, transcendentals=0
        )
    return pl.pallas_call(
        kernel,
        out_shape=outs,
        in_specs=[ANY if at in in_any else VMEM for at in range(len(operands))],
        out_specs=tuple(ANY if at in out_any else VMEM for at in range(len(outs))),
        scratch_shapes=scratch,
        compiler_params=pltpu.CompilerParams(vmem_limit_bytes=limit * 2**20),
        cost_estimate=cost,
        name=name,
    )(*operands)


def gather_weights(weights):
    taps_first = jnp.transpose(weights, (1, 0, 2)).reshape(TAPS * BLOCK, BLOCK)
    (own,) = call(
        transpose_kernel, "weights_transpose", (shape(BLOCK, COLS),), [], 0, [taps_first]
    )
    beside = [lax.ppermute(own, "slab", to_z(k)) for k in range(1, ZN)]
    pieces = along_y(own)
    line = jnp.concatenate(beside, axis=0)
    return pieces + along_y(once(line, pieces[2], pieces[3]))


def once(value, *others):
    return lax.optimization_barrier((value, *others))[0]


def along_y(line):
    half = line.shape[0] // 2
    before = lax.ppermute(line, "slab", to_y(1))
    after = lax.ppermute(line, "slab", to_y(-1))
    first = lax.ppermute(before[:half], "slab", to_y(1))
    second = lax.ppermute(after[half:], "slab", to_y(-1))
    return [line, before, first, second, after]


def gather_inputs(inputs, w_pieces):
    far = lax.ppermute(once(inputs, w_pieces[5]), "filt", TO_ZHI)
    pair = jnp.concatenate([inputs, far], axis=0)
    row = jnp.concatenate(
        [pair] + [lax.ppermute(pair, "filt", to_x(k)) for k in range(1, XN)], axis=0
    )
    return [row, lax.ppermute(row, "filt", TO_CORE)]


def sum_over_row(part):
    size = part.shape[0] // 2
    received = lax.ppermute(part[size:], "filt", TO_CORE)
    sums = []
    for k in range(XN):
        rows = slice(k * BLOCK, (k + 1) * BLOCK)
        sums.append((part[rows].astype(F32) + received[rows].astype(F32)).astype(BF16))
    arrived = [lax.ppermute(sums[k], "filt", to_x(k)) for k in range(1, XN)]
    result = sums[0].astype(F32)
    for piece in arrived:
        result = result + piece.astype(F32)
    return result


def local(inputs, weights, bias, cotangent):
    w_pieces = gather_weights(weights)
    x_pieces = gather_inputs(inputs.reshape(BLOCK, CELLS), w_pieces)
    (ready,) = call(
        ready_kernel, "weights_ready", (shape(8, 128),), [], 7168, w_pieces[7:9], in_any=range(2)
    )
    same_taps, beside_taps, up, down = call(
        forward_beside_kernel,
        "forward_beside",
        (
            shape(CHANNELS, SAME),
            shape(CHANNELS, BESIDE),
            shape(BLOCK, CELLS),
            shape(BLOCK, CELLS),
        ),
        [
            pltpu.VMEM((CHANNELS, CELLS), BF16),
            pltpu.VMEM((CHANNELS, BESIDE), BF16),
            pltpu.VMEM((BESIDE, CELLS), F32),
            pltpu.SemaphoreType.DMA,
        ],
        BESIDE,
        x_pieces + w_pieces + [ready],
        in_any=(12,),
        out_any=(1,),
        limit=46,
    )
    below = lax.ppermute(up, "slab", UP)
    above = lax.ppermute(down, "slab", DOWN)
    (own,) = call(
        forward_same_kernel,
        "forward_same",
        (shape(BLOCK, CELLS, F32),),
        [pltpu.VMEM((CHANNELS, CELLS), BF16), pltpu.VMEM((SAME, CELLS), F32)],
        SAME,
        x_pieces + [same_taps],
    )
    activated, grad = call(
        pointwise_kernel,
        "silu_and_slope",
        (shape(BLOCK, CELLS), shape(BLOCK, CELLS)),
        [],
        0,
        [own, below, above, bias.reshape(BLOCK, 1), cotangent.reshape(BLOCK, CELLS)],
    )
    grad_below = lax.ppermute(grad, "slab", UP)
    grad_above = lax.ppermute(grad, "slab", DOWN)
    (same,) = call(
        backward_same_kernel,
        "backward_same",
        (shape(CHANNELS, CELLS, F32),),
        [pltpu.VMEM((SAME, CELLS), BF16)],
        SAME,
        [grad, same_taps],
    )
    far, stacked = call(
        backward_far_kernel,
        "backward_far",
        (shape(CHANNELS // 2, CELLS), shape(BESIDE, CELLS)),
        [],
        BESIDE // 2,
        [grad_above, grad_below, same, beside_taps],
    )
    (near,) = call(
        backward_near_kernel,
        "backward_near",
        (shape(CHANNELS // 2, CELLS),),
        [],
        BESIDE // 2,
        [stacked, same, beside_taps],
    )
    far, near = sum_over_row(far), sum_over_row(near)
    arrived = lax.ppermute(far.astype(BF16), "filt", TO_ZHI)
    input_grad = (near + arrived.astype(F32)).astype(BF16)
    return activated.reshape(cotangent.shape), input_grad.reshape(inputs.shape)


def solution(mesh):
    return jax.shard_map(
        local,
        mesh=mesh,
        in_specs=(
            P("filt", "slab", None),
            P("filt", None, "slab"),
            P("filt"),
            P("filt", "slab", None),
        ),
        out_specs=(P("filt", "slab", None), P("filt", "slab", None)),
        check_vma=False,
    )
```

```python
import jax
import jax.numpy as jnp
from jax import lax
from jax.experimental import pallas as pl
from jax.experimental.pallas import tpu as pltpu
from jax.sharding import PartitionSpec as P

HH = 32
WW = 32
CELLS = HH * WW
TAPS = 27
SLOT_TAPS = [*range(9, 18), None, *range(0, 9), *range(18, 27)]
SLOTS = 28
BLOCK = 64
COLS = SLOTS * BLOCK
SAME = 10 * BLOCK
BESIDE = COLS - SAME
BLOCKS = 16
CHANNELS = BLOCKS * BLOCK

ZH, XN, CN = 2, 4, 2
YN, ZN = 4, 4

BF16 = jnp.bfloat16
F32 = jnp.float32


def filt_index(zh, x, c):
    return (zh * XN + x) * CN + c


FILT = [(zh, x, c) for zh in range(ZH) for x in range(XN) for c in range(CN)]
SLAB = [(y, z) for y in range(YN) for z in range(ZN)]
TO_CORE = [(filt_index(*d), filt_index(d[0], d[1], 1 - d[2])) for d in FILT]
TO_ZHI = [(filt_index(*d), filt_index(1 - d[0], d[1], d[2])) for d in FILT]


def to_x(k):
    return [(filt_index(*d), filt_index(d[0], (d[1] + k) % XN, d[2])) for d in FILT]


def to_y(k):
    return [(y * ZN + z, ((y + k) % YN) * ZN + z) for y, z in SLAB]


def to_z(k):
    return [(y * ZN + z, y * ZN + (z + k) % ZN) for y, z in SLAB]


UP = [(i, i + 1) for i in range(YN * ZN - 1)]
DOWN = [(i + 1, i) for i in range(YN * ZN - 1)]

VMEM = pl.BlockSpec(memory_space=pltpu.VMEM)
ANY = pl.BlockSpec(memory_space=pl.ANY)


def transpose_kernel(w_ref, out_ref):
    for pair in range(0, SLOTS, 2):
        parts = []
        for slot in (pair, pair + 1):
            tap = SLOT_TAPS[slot]
            if tap is None:
                parts.append(jnp.zeros((BLOCK, BLOCK), F32))
            else:
                parts.append(w_ref[tap * BLOCK : (tap + 1) * BLOCK, :].astype(F32))
        turned = jnp.concatenate(parts, axis=0).T
        out_ref[:, pair * BLOCK : (pair + 2) * BLOCK] = turned.astype(BF16)


def filt_position():
    mine = lax.axis_index("filt")
    return mine // (XN * CN), (mine // CN) % XN, mine % CN


def slab_position():
    mine = lax.axis_index("slab")
    return mine // ZN, mine % ZN


def rows_of(block):
    return pl.ds(pl.multiple_of(block * BLOCK, BLOCK), BLOCK)


def assemble_weights(pieces, same_ref, beside_ref):
    y, z = slab_position()
    half = BLOCK // 2
    for step_y in range(YN):
        for step_z in range(ZN):
            block = ((y + YN - step_y) % YN) * ZN + (z + ZN - step_z) % ZN
            for part in range(2):
                start = part * half
                if step_z == 0:
                    ref = pieces[step_y]
                else:
                    start += (step_z - 1) * BLOCK
                    if step_y == 2:
                        ref = pieces[YN + (2 if start < 3 * half else 3)]
                        start %= 3 * half
                    else:
                        ref = pieces[YN + {0: 0, 1: 1, 3: 4}[step_y]]
                rows = pl.ds(pl.multiple_of(block * BLOCK + part * half, half), half)
                same_ref[rows, :] = ref[start : start + half, :SAME]
                beside_ref[rows, :] = ref[start : start + half, SAME:]


def assemble_inputs(pieces, x_ref):
    zh, x, c = filt_position()
    for other in range(CN):
        for step in range(XN):
            for far in range(ZH):
                core = c if other == 0 else 1 - c
                high = zh if far == 0 else 1 - zh
                block = filt_index(high, (x + XN - step) % XN, core)
                start = (step * ZH + far) * BLOCK
                x_ref[rows_of(block), :] = pieces[other][start : start + BLOCK, :]


def shifted_sum(y_scr, first, base):
    cell = lax.broadcasted_iota(jnp.int32, (8, CELLS), 1)
    column = cell % WW
    row_ok = {0: cell >= WW, 2: cell < CELLS - WW}
    col_ok = {0: column >= 1, 2: column < WW - 1}
    total = None
    for col in range(3):
        lane = None
        for row in range(3):
            value = y_scr[pl.ds((first + 3 * row + col) * BLOCK + base, 8), :]
            if row != 1:
                value = pltpu.roll(value, ((1 - row) * WW) % CELLS, 1)
                value = jnp.where(row_ok[row], value, 0.0)
            lane = value if lane is None else lane + value
        if col != 1:
            lane = pltpu.roll(lane, (1 - col) % CELLS, 1)
            lane = jnp.where(col_ok[col], lane, 0.0)
        total = lane if total is None else total + lane
    return total


def convolve(planes, w, x, out_refs, y_scr):
    y_scr[...] = lax.dot_general(w, x, (((0,), (0,)), ((), ())), preferred_element_type=F32)

    def body(part, carry):
        base = pl.multiple_of(part * 8, 8)
        for first, out in zip(planes, out_refs):
            out[pl.ds(base, 8), :] = shifted_sum(y_scr, first, base).astype(out.dtype)
        return carry

    lax.fori_loop(0, BLOCK // 8, body, 0)


def forward_beside_kernel(*refs):
    x_pieces, w_pieces = refs[:2], refs[2:11]
    same_ref, beside_ref, up_ref, down_ref, x_scr, w_scr, y_scr, sem = refs[12:]
    assemble_inputs(x_pieces, x_scr)
    assemble_weights(w_pieces, same_ref, w_scr)
    keep = pltpu.make_async_copy(w_scr, beside_ref, sem)
    keep.start()
    convolve((0, 9), w_scr[...], x_scr[...], (up_ref, down_ref), y_scr)
    keep.wait()


def ready_kernel(*refs):
    refs[-1][...] = jnp.zeros((8, 128), BF16)


def forward_same_kernel(first_ref, second_ref, same_ref, own_ref, x_scr, y_scr):
    assemble_inputs((first_ref, second_ref), x_scr)
    convolve((0,), same_ref[...], x_scr[...], (own_ref,), y_scr)


def pointwise_kernel(own_ref, below_ref, above_ref, bias_ref, cot_ref, act_ref, grad_ref):
    preact = (
        own_ref[...]
        + below_ref[...].astype(F32)
        + above_ref[...].astype(F32)
        + bias_ref[...].astype(F32)
    )
    sig = jax.nn.sigmoid(preact)
    act_ref[...] = (preact * sig).astype(BF16)
    slope = sig * (1.0 + preact * (1.0 - sig))
    grad_ref[...] = (cot_ref[...].astype(F32) * slope).astype(BF16)


def stack_taps(grad_refs, g_scr):
    cell = lax.broadcasted_iota(jnp.int32, (16, CELLS), 1)
    column = cell % WW
    row_ok = {2: cell >= WW, 0: cell < CELLS - WW}
    col_ok = {2: column >= 1, 0: column < WW - 1}

    def body(part, carry):
        base = pl.multiple_of(part * 16, 16)
        for at, grad in enumerate(grad_refs):
            plane = grad[pl.ds(base, 16), :].astype(F32)
            for col in range(3):
                lane = plane
                if col != 1:
                    lane = pltpu.roll(lane, (col - 1) % CELLS, 1)
                    lane = jnp.where(col_ok[col], lane, 0.0)
                for row in range(3):
                    value = lane
                    if row != 1:
                        value = pltpu.roll(value, ((row - 1) * WW) % CELLS, 1)
                        value = jnp.where(row_ok[row], value, 0.0)
                    slot = 9 * at + 3 * row + col
                    g_scr[pl.ds(slot * BLOCK + base, 16), :] = value.astype(BF16)
        return carry

    lax.fori_loop(0, BLOCK // 16, body, 0)


def backward_same_kernel(grad_ref, w_ref, out_ref, g_scr):
    stack_taps([grad_ref], g_scr)
    g_scr[9 * BLOCK :, :] = jnp.zeros((BLOCK, CELLS), BF16)
    half = CHANNELS // 2
    for start in (0, half):
        out_ref[start : start + half, :] = jnp.dot(
            w_ref[start : start + half, :], g_scr[...], preferred_element_type=F32
        )


def backward_far_kernel(above_ref, below_ref, same_ref, w_ref, out_ref, g_ref):
    stack_taps([above_ref, below_ref], g_ref)
    backward_rows(1, g_ref, same_ref, w_ref, out_ref)


def backward_near_kernel(g_ref, same_ref, w_ref, out_ref):
    backward_rows(0, g_ref, same_ref, w_ref, out_ref)


def backward_rows(far, g_ref, same_ref, w_ref, out_ref):
    zh, x, c = filt_position()
    size = CHANNELS // 2
    first = pl.multiple_of(((zh + far) % ZH) * size, size)
    total = same_ref[pl.ds(first, size), :] + jnp.dot(
        w_ref[pl.ds(first, size), :], g_ref[...], preferred_element_type=F32
    )
    total = total.astype(BF16)
    for at in range(size // BLOCK):
        along, core = at // CN, at % CN
        place = (core + c) % CN * XN + (along + XN - x) % XN
        out_ref[rows_of(place), :] = total[at * BLOCK : (at + 1) * BLOCK, :]


def shape(rows, columns, dtype=BF16):
    return jax.ShapeDtypeStruct((rows, columns), dtype)


def call(kernel, name, outs, scratch, columns, operands, in_any=(), out_any=(), limit=24):
    cost = None
    if columns:
        cost = pl.CostEstimate(
            flops=2 * columns * CHANNELS * CELLS, bytes_accessed=2**20, transcendentals=0
        )
    return pl.pallas_call(
        kernel,
        out_shape=outs,
        in_specs=[ANY if at in in_any else VMEM for at in range(len(operands))],
        out_specs=tuple(ANY if at in out_any else VMEM for at in range(len(outs))),
        scratch_shapes=scratch,
        compiler_params=pltpu.CompilerParams(vmem_limit_bytes=limit * 2**20),
        cost_estimate=cost,
        name=name,
    )(*operands)


def gather_weights(weights):
    taps_first = jnp.transpose(weights, (1, 0, 2)).reshape(TAPS * BLOCK, BLOCK)
    (own,) = call(
        transpose_kernel, "weights_transpose", (shape(BLOCK, COLS),), [], 0, [taps_first]
    )
    beside = [lax.ppermute(own, "slab", to_z(k)) for k in range(1, ZN)]
    pieces = [own] + [lax.ppermute(own, "slab", to_y(k)) for k in range(1, YN)]
    line = jnp.concatenate(beside, axis=0)
    return pieces + along_y(once(line, pieces[1], pieces[3]))


def once(value, *others):
    return lax.optimization_barrier((value, *others))[0]


def along_y(line):
    half = line.shape[0] // 2
    before = lax.ppermute(line, "slab", to_y(1))
    after = lax.ppermute(line, "slab", to_y(-1))
    first = lax.ppermute(before[:half], "slab", to_y(1))
    second = lax.ppermute(after[half:], "slab", to_y(-1))
    return [line, before, first, second, after]


def gather_inputs(inputs, w_pieces):
    far = lax.ppermute(once(inputs, w_pieces[4], w_pieces[2]), "filt", TO_ZHI)
    pair = jnp.concatenate([inputs, far], axis=0)
    row = jnp.concatenate(
        [pair] + [lax.ppermute(pair, "filt", to_x(k)) for k in range(1, XN)], axis=0
    )
    return [row, lax.ppermute(row, "filt", TO_CORE)]


def sum_over_row(part):
    size = part.shape[0] // 2
    received = lax.ppermute(part[size:], "filt", TO_CORE)
    sums = []
    for k in range(XN):
        rows = slice(k * BLOCK, (k + 1) * BLOCK)
        sums.append((part[rows].astype(F32) + received[rows].astype(F32)).astype(BF16))
    arrived = [lax.ppermute(sums[k], "filt", to_x(k)) for k in range(1, XN)]
    result = sums[0].astype(F32)
    for piece in arrived:
        result = result + piece.astype(F32)
    return result


def local(inputs, weights, bias, cotangent):
    w_pieces = gather_weights(weights)
    x_pieces = gather_inputs(inputs.reshape(BLOCK, CELLS), w_pieces)
    (ready,) = call(
        ready_kernel, "weights_ready", (shape(8, 128),), [], 7168, w_pieces[6:8], in_any=range(2)
    )
    same_taps, beside_taps, up, down = call(
        forward_beside_kernel,
        "forward_beside",
        (
            shape(CHANNELS, SAME),
            shape(CHANNELS, BESIDE),
            shape(BLOCK, CELLS),
            shape(BLOCK, CELLS),
        ),
        [
            pltpu.VMEM((CHANNELS, CELLS), BF16),
            pltpu.VMEM((CHANNELS, BESIDE), BF16),
            pltpu.VMEM((BESIDE, CELLS), F32),
            pltpu.SemaphoreType.DMA,
        ],
        BESIDE,
        x_pieces + w_pieces + [ready],
        in_any=(11,),
        out_any=(1,),
        limit=46,
    )
    below = lax.ppermute(up, "slab", UP)
    above = lax.ppermute(down, "slab", DOWN)
    (own,) = call(
        forward_same_kernel,
        "forward_same",
        (shape(BLOCK, CELLS, F32),),
        [pltpu.VMEM((CHANNELS, CELLS), BF16), pltpu.VMEM((SAME, CELLS), F32)],
        SAME,
        x_pieces + [same_taps],
    )
    activated, grad = call(
        pointwise_kernel,
        "silu_and_slope",
        (shape(BLOCK, CELLS), shape(BLOCK, CELLS)),
        [],
        0,
        [own, below, above, bias.reshape(BLOCK, 1), cotangent.reshape(BLOCK, CELLS)],
    )
    grad_below = lax.ppermute(grad, "slab", UP)
    grad_above = lax.ppermute(grad, "slab", DOWN)
    (same,) = call(
        backward_same_kernel,
        "backward_same",
        (shape(CHANNELS, CELLS, F32),),
        [pltpu.VMEM((SAME, CELLS), BF16)],
        SAME,
        [grad, same_taps],
    )
    far, stacked = call(
        backward_far_kernel,
        "backward_far",
        (shape(CHANNELS // 2, CELLS), shape(BESIDE, CELLS)),
        [],
        BESIDE // 2,
        [grad_above, grad_below, same, beside_taps],
    )
    (near,) = call(
        backward_near_kernel,
        "backward_near",
        (shape(CHANNELS // 2, CELLS),),
        [],
        BESIDE // 2,
        [stacked, same, beside_taps],
    )
    far, near = sum_over_row(far), sum_over_row(near)
    arrived = lax.ppermute(far.astype(BF16), "filt", TO_ZHI)
    input_grad = (near + arrived.astype(F32)).astype(BF16)
    return activated.reshape(cotangent.shape), input_grad.reshape(inputs.shape)


def solution(mesh):
    return jax.shard_map(
        local,
        mesh=mesh,
        in_specs=(
            P("filt", "slab", None),
            P("filt", None, "slab"),
            P("filt"),
            P("filt", "slab", None),
        ),
        out_specs=(P("filt", "slab", None), P("filt", "slab", None)),
        check_vma=False,
    )
```
